128 devices in a mesh: aa: 8 (over x_hi, z), ba: 16 (over x_lo, y, core).
Axes of the slice: x: 4 (x_hi: 2, x_lo: 2; x = x_hi * 2 + x_lo), y: 4, z: 4, core: 2. Of those that a mesh axis runs over, the one named last changes fastest.
Arguments:
- feats: bfloat16 [8, 64, 128, 256], P('aa', 'ba'), may hold values from -6 to 6
- conv_one: bfloat16 [3, 3, 3, 256, 256], replicated, may hold values from -0.078125 to 0.078125
- bias_one: float32 [256], replicated, may hold values from -3 to 3
- conv_two: bfloat16 [3, 3, 3, 256, 256], replicated, may hold values from -0.078125 to 0.078125
- bias_two: float32 [256], replicated, may hold values from -3 to 3
- patch_weight: bfloat16 [2, 2, 256, 128], replicated, may hold values from -0.1875 to 0.1875
- patch_bias: float32 [128], replicated, may hold values from -3 to 3
- embed_weight: bfloat16 [128, 2048], replicated, may hold values from -0.5 to 0.5
- embed_bias: float32 [2048], replicated, may hold values from -6 to 6
- norm_gain: float32 [2048], replicated, may hold values from 0.1 to 1.9
- w_query: bfloat16 [2048, 2048], P(None, 'ba'), may hold values from -2 to 2
- w_key: bfloat16 [2048, 2048], P(None, 'ba'), may hold values from -2 to 2
- w_value: bfloat16 [2048, 2048], P(None, 'ba'), may hold values from -0.125 to 0.125
- w_velocity: bfloat16 [2048, 128], P('ba'), may hold values from -0.5 to 0.5
Outputs:
- velocity: float32 [16384, 128], P(('aa', 'ba'))
The draws below stay inside these ranges and needn't reach their ends.
All inputs are finite; a program needn't handle non-finite values.
Results may differ from the reference program's by a relative error of at most 0.035.
Values may be sent and summed in bfloat16 or wider, within the bound.
No kernel may reach another device: no remote copies, remote signals or barrier semaphores. Data moves between devices by JAX's collectives and lax.ppermute only.
A program may use at most 128 MiB of HBM per device.

```python
import math
import jax
import jax.numpy as jnp
from jax import lax

C = 256
LAT = 128
D = 2048
HEADS = 32
HEAD_DIM = 64
FT = 1
SH = 4
W = 128
TOKENS = 16384
FRAMES = 8
ROWS = 64
N_AA = 8
N_BA = 16


def shared_query(key):
    return jax.random.normal(jax.random.fold_in(key, 11), (D, D), jnp.float32) * D ** (-0.5)


def draw_w_query(key, part):
    return jnp.clip(shared_query(key), -2.0, 2.0).astype(jnp.bfloat16)


def draw_w_key(key, part):
    noise = jax.random.normal(jax.random.fold_in(key, 23), (D, D), jnp.float32) * (4.0 * D ** (-0.5))
    return jnp.clip(noise, -2.0, 2.0).astype(jnp.bfloat16)


def levels(own_key, dims, cuts, smallest, high):
    def one(axis_at, blocks):
        draws = jax.random.uniform(jax.random.fold_in(jax.random.fold_in(own_key, 6), axis_at), (blocks,), jnp.float32, smallest / len(cuts), high / len(cuts))
        return jnp.repeat(jnp.exp(draws), dims[axis_at] // blocks).reshape((-1,) + (1,) * (len(dims) - axis_at - 1))

    gain = one(*cuts[0])
    for cut in cuts[1:]:
        gain = gain * one(*cut)
    return gain


def scatter_about(own_key, extent, deviation, reach, cuts=(), dtype=jnp.bfloat16):
    values = deviation * jax.random.normal(own_key, extent, jnp.float32)
    if cuts:
        values = values * levels(own_key, extent, cuts, -0.22, 0.18)
    return jnp.clip(values, -reach, reach).astype(dtype)


def setup_inputs(seed: int = 0) -> dict:
    key_list = jax.random.split(jax.random.key(seed), 15)
    return {
        "feats": scatter_about(key_list[0], (FRAMES, ROWS, W, C), 1.0, 6.0, ((0, 8), (1, 16))),
        "conv_one": scatter_about(key_list[1], (3, 3, 3, C, C), (27 * C) ** -0.5, 0.078125),
        "bias_one": scatter_about(key_list[2], (C,), 0.5, 3.0, (), jnp.float32),
        "conv_two": scatter_about(key_list[3], (3, 3, 3, C, C), (27 * C) ** -0.5, 0.078125),
        "bias_two": scatter_about(key_list[4], (C,), 0.5, 3.0, (), jnp.float32),
        "patch_weight": scatter_about(key_list[5], (2, 2, C, LAT), (4 * C) ** -0.5, 0.1875),
        "patch_bias": scatter_about(key_list[6], (LAT,), 0.5, 3.0, (), jnp.float32),
        "embed_weight": scatter_about(key_list[7], (LAT, D), LAT ** -0.5, 0.5),
        "embed_bias": scatter_about(key_list[8], (D,), 1.0, 6.0, (), jnp.float32),
        "norm_gain": jnp.clip(1.0 + 0.18 * jax.random.normal(key_list[9], (D,), jnp.float32), 0.1, 1.9),
        "w_query": draw_w_query(jax.random.fold_in(key_list[14], 71), 0),
        "w_key": draw_w_key(jax.random.fold_in(key_list[14], 71), 0),
        "w_value": scatter_about(key_list[12], (D, D), D ** -0.5, 0.125, ((1, 16),)),
        "w_velocity": scatter_about(key_list[13], (D, LAT), (D // 16) ** -0.5, 0.5, ((0, 16),)),
    }


def convolve(field, kernel, bias):
    frames, rows, width, chans = field.shape
    padded = jnp.pad(field, ((1, 1), (1, 1), (1, 1), (0, 0)))
    total = jnp.zeros((frames * rows * width, kernel.shape[-1]), jnp.float32)
    for shift_t in range(3):
        for shift_r in range(3):
            window = padded[shift_t:shift_t + frames, shift_r:shift_r + rows]
            stacked = jnp.concatenate([window[:, :, shift_w:shift_w + width] for shift_w in range(3)], axis=-1)
            total = total + jnp.dot(stacked.reshape(-1, 3 * chans), kernel[shift_t, shift_r].reshape(3 * chans, -1), preferred_element_type=jnp.float32)
    return (total + bias).reshape(frames, rows, width, -1)

def patchify(field, weight, bias):
    frames, rows, width, chans = field.shape
    blocks = field.reshape(frames, rows // 2, 2, width // 2, 2, chans).transpose(0, 1, 3, 2, 4, 5).reshape(-1, 4 * chans)
    return (jnp.dot(blocks, weight.reshape(4 * chans, -1), preferred_element_type=jnp.float32) + bias).astype(jnp.bfloat16)

def normalize(latent_rows, embed_weight, embed_bias, norm_gain):
    hidden = jnp.dot(latent_rows, embed_weight, preferred_element_type=jnp.float32) + embed_bias
    center = hidden - hidden.mean(-1, keepdims=True)
    spread = (center * center).mean(-1, keepdims=True)
    return (center * lax.rsqrt(spread + 1e-05) * norm_gain).astype(jnp.bfloat16)

def head_attention(trio):
    query_head, key_head, value_head = trio
    scale = HEAD_DIM ** (-0.5)
    count = math.gcd(TOKENS, 1024)

    def one_block(query_block):
        scores = jnp.dot(query_block, key_head.T, preferred_element_type=jnp.float32) * scale
        probs = jnp.exp(scores - scores.max(-1, keepdims=True))
        denom = probs.sum(-1, keepdims=True)
        return (jnp.dot(probs.astype(jnp.bfloat16), value_head, preferred_element_type=jnp.float32) / denom).astype(jnp.bfloat16)
    return lax.map(one_block, query_head.reshape(-1, count, HEAD_DIM)).reshape(TOKENS, HEAD_DIM)

def reference(feats, conv_one, bias_one, conv_two, bias_two, patch_weight, patch_bias, embed_weight, embed_bias, norm_gain, w_query, w_key, w_value, w_velocity):
    first = jax.nn.gelu(convolve(feats, conv_one, bias_one), approximate=False).astype(jnp.bfloat16)
    second = (first.astype(jnp.float32) + jax.nn.gelu(convolve(first, conv_two, bias_two), approximate=False)).astype(jnp.bfloat16)
    patches = patchify(second, patch_weight, patch_bias)
    latents = patches.reshape(N_AA, FT, N_BA, SH // 2, W // 2, LAT).transpose(0, 2, 1, 3, 4, 5).reshape(TOKENS, LAT)
    normed = normalize(latents, embed_weight, embed_bias, norm_gain)
    queries = jnp.dot(normed, w_query, preferred_element_type=jnp.float32).astype(jnp.bfloat16)
    keys = jnp.dot(normed, w_key, preferred_element_type=jnp.float32).astype(jnp.bfloat16)
    values = jnp.dot(normed, w_value, preferred_element_type=jnp.float32).astype(jnp.bfloat16)

    def split_heads(matrix):
        return matrix.reshape(TOKENS, HEADS, HEAD_DIM).transpose(1, 0, 2)
    attended = lax.map(head_attention, (split_heads(queries), split_heads(keys), split_heads(values)))
    attended = attended.transpose(1, 0, 2).reshape(TOKENS, D)
    return jnp.dot(attended, w_velocity, preferred_element_type=jnp.float32)
```

```python
import functools
import math

import jax
import jax.numpy as jnp
from jax import lax
from jax.experimental import pallas as pl
from jax.experimental.pallas import tpu as pltpu
from jax.sharding import PartitionSpec as P

HEAD_DIM = 64
BF = jnp.bfloat16
F32 = jnp.float32
DEPTH = 144
TILE = 128
SAMPLE = 2
MIB = 2**20
TN = (((0,), (0,)), ((), ()))
HI = lax.Precision.HIGHEST


def gelu(x):
    return 0.5 * x * (1.0 + lax.erf(x * (1.0 / math.sqrt(2.0))))


def neighbours(block, row_axis):
    na, nb = lax.axis_size("aa"), lax.axis_size("ba")

    def shift(x, da, db):
        pairs = []
        for a in range(na):
            for b in range(nb):
                if 0 <= a + da < na and 0 <= b + db < nb:
                    pairs.append((a * nb + b, (a + da) * nb + b + db))
        return lax.ppermute(x, ("aa", "ba"), pairs)

    top, bottom = block[:1], block[-1:]
    before = shift(block, 1, 0)
    after = shift(block, -1, 0)
    ups = [shift(bottom, da, 1) for da in (1, 0, -1)]
    downs = [shift(top, da, -1) for da in (1, 0, -1)]
    return (before, block, after, *ups, *downs)


def conv_taps(refs, w_ref, pad_ref, acc_ref):
    step = pl.program_id(0)
    rows, width, chans = refs[1].shape

    @pl.when(step == 0)
    def _():
        for t in range(3):
            pad_ref[t, 0:width] = refs[3 + t][0]
            for r in range(rows):
                pad_ref[t, (r + 1) * width : (r + 2) * width] = refs[t][r]
            pad_ref[t, (rows + 1) * width : (rows + 2) * width] = refs[6 + t][0]

    for w in range(3):
        total = jnp.dot(pad_ref[step, 0 : rows * width], w_ref[0, 0, w], preferred_element_type=F32)
        for r in (1, 2):
            total += jnp.dot(
                pad_ref[step, r * width : (r + rows) * width],
                w_ref[0, r, w],
                preferred_element_type=F32,
            )

        @pl.when(step == 0)
        def _():
            acc_ref[w] = total

        @pl.when(step > 0)
        def _():
            acc_ref[w] += total


def conv_sum(acc_ref, bias_ref, width):
    count = acc_ref.shape[1]
    at = lax.broadcasted_iota(jnp.int32, (count, 1), 0) % width
    left = jnp.where(at == 0, 0.0, pltpu.roll(acc_ref[0], 1, 0))
    right = jnp.where(at == width - 1, 0.0, pltpu.roll(acc_ref[2], count - 1, 0))
    return left + acc_ref[1] + right + bias_ref[...]


def first_kernel(*refs):
    halo, (w_ref, bias_ref, out_ref, pad_ref, acc_ref) = refs[:9], refs[9:]
    conv_taps(halo, w_ref, pad_ref, acc_ref)

    @pl.when(pl.program_id(0) == 2)
    def _():
        rows, width, chans = out_ref.shape
        out_ref[...] = gelu(conv_sum(acc_ref, bias_ref, width)).astype(BF).reshape(rows, width, chans)


def second_kernel(*refs):
    halo, (w_ref, bias_ref, pw_ref, pb_ref, out_ref, pad_ref, acc_ref) = refs[:9], refs[9:]
    conv_taps(halo, w_ref, pad_ref, acc_ref)

    @pl.when(pl.program_id(0) == 2)
    def _():
        rows, width, chans = halo[1].shape
        half = width // 2
        first = halo[1][...].reshape(rows * width, chans).astype(F32)
        second = (first + gelu(conv_sum(acc_ref, bias_ref, width))).astype(BF)
        r = lax.broadcasted_iota(jnp.int32, (width, width), 0)
        c = lax.broadcasted_iota(jnp.int32, (width, width), 1)
        picks = (c == jnp.where(r < half, 2 * r, 2 * r - (width - 1))).astype(BF)
        for e in range(rows // 2):
            total = pb_ref[...] + jnp.zeros((half, pb_ref.shape[1]), F32)
            for a in range(2):
                at = (2 * e + a) * width
                sorted_row = jnp.dot(
                    picks, second[at : at + width], preferred_element_type=F32
                ).astype(BF)
                for k in range(2):
                    total += jnp.dot(
                        sorted_row[k * half : (k + 1) * half],
                        pw_ref[a, k],
                        preferred_element_type=F32,
                    )
            out_ref[e * half : (e + 1) * half] = total.astype(BF)


def conv_call(kernel, halo, weight, extras, out_shape):
    rows, width, chans = halo[1].shape
    whole = [pl.BlockSpec(memory_space=pltpu.VMEM)]
    return pl.pallas_call(
        kernel,
        grid=(3,),
        in_specs=whole * 9
        + [pl.BlockSpec((1, 3, 3, chans, chans), lambda i: (i, 0, 0, 0, 0))]
        + whole * len(extras),
        out_specs=pl.BlockSpec(memory_space=pltpu.VMEM),
        out_shape=jax.ShapeDtypeStruct(out_shape, BF),
        scratch_shapes=[
            pltpu.VMEM((3, (rows + 2) * width, chans), BF),
            pltpu.VMEM((3, rows * width, chans), F32),
        ],
        compiler_params=pltpu.CompilerParams(vmem_limit_bytes=32 * MIB),
        cost_estimate=pl.CostEstimate(
            flops=2 * 27 * rows * width * chans * chans,
            bytes_accessed=2 * 27 * chans * chans,
            transcendentals=0,
        ),
    )(*halo, weight, *extras)


def side(tiles):
    return jnp.concatenate(tiles, axis=1)


def attend_kernel(n_blocks, start, finish, heads, *refs):
    q_ref, *rest = refs
    blocks, rest = rest[:n_blocks], rest[n_blocks:]
    if not start:
        (m_in, o_in, *rest) = rest
    if finish:
        n_all = len(rest) - 3
        everything, (out_ref, held, sem) = rest[:n_all], rest[n_all:]
    else:
        m_out, out_ref = rest
    query = side([q_ref[h] for h in range(heads)])

    def scores(tiles):
        return lax.dot_general(tiles, query, TN, preferred_element_type=F32)

    if start:
        sample = side([blocks[0][i] for i in range(SAMPLE)])
        shift = scores(sample).max(0, keepdims=True)
        total = jnp.zeros((DEPTH, heads * TILE), F32)
    else:
        shift = m_in[...]
        total = side([o_in[h] for h in range(heads)])
    for block in blocks:
        keys = side([block[i] for i in range(block.shape[0])])
        probs = jnp.exp2(scores(keys) - shift).astype(BF)
        total = total + jnp.dot(keys, probs, preferred_element_type=F32)
    if not finish:
        m_out[...] = shift
        for h in range(heads):
            out_ref[h] = total[:, h * TILE : (h + 1) * TILE]
        return

    def store(sums):
        scaled = (sums / sums[TILE + 1 : TILE + 2]).astype(BF)
        for h in range(heads):
            out_ref[h] = scaled[:, h * TILE : (h + 1) * TILE]

    store(total)
    largest = jnp.where(total[TILE + 1 : TILE + 2] < 2.0**100, 0.0, 1.0).max()

    @pl.when(largest > 0.5)
    def _():
        state = (
            jnp.full((1, heads * TILE), -1e38, F32),
            jnp.zeros((DEPTH, heads * TILE), F32),
        )
        for source in everything:
            copy = pltpu.make_async_copy(source, held, sem)
            copy.start()
            copy.wait()

            def one_tile(i, state):
                best, sums = state
                keys = held[i]
                s = scores(keys)
                peak = jnp.maximum(best, s.max(0, keepdims=True))
                probs = jnp.exp2(s - peak).astype(BF)
                sums = sums * jnp.exp2(best - peak) + jnp.dot(
                    keys, probs, preferred_element_type=F32
                )
                return peak, sums

            state = lax.fori_loop(0, held.shape[0], one_tile, state)
        store(state[1])


def attend_call(queries, blocks, state, everything, heads):
    n_heads = queries.shape[0]
    start, finish = state is None, everything is not None
    per_q = pl.BlockSpec((heads, DEPTH, TILE), lambda i: (i, 0, 0))
    per_m = pl.BlockSpec((1, heads * TILE), lambda i: (0, i))
    whole = pl.BlockSpec(memory_space=pltpu.VMEM)
    args, specs = [queries, *blocks], [per_q] + [whole] * len(blocks)
    if not start:
        args += state
        specs += [per_m, per_q]
    scratch = []
    if finish:
        args += everything
        specs += [pl.BlockSpec(memory_space=pl.ANY)] * len(everything)
        out_specs = per_q
        out_shape = jax.ShapeDtypeStruct(queries.shape, BF)
        scratch = [pltpu.VMEM(blocks[0].shape, BF), pltpu.SemaphoreType.DMA(())]
    else:
        out_specs = [per_m, per_q]
        out_shape = [
            jax.ShapeDtypeStruct((1, n_heads * TILE), F32),
            jax.ShapeDtypeStruct(queries.shape, F32),
        ]
    pairs = n_heads * TILE * sum(b.shape[0] for b in blocks) * TILE
    return pl.pallas_call(
        functools.partial(attend_kernel, len(blocks), start, finish, heads),
        grid=(n_heads // heads,),
        in_specs=specs,
        out_specs=out_specs,
        out_shape=out_shape,
        scratch_shapes=scratch,
        compiler_params=pltpu.CompilerParams(vmem_limit_bytes=58 * MIB),
        cost_estimate=pl.CostEstimate(
            flops=pairs * 1024, bytes_accessed=4 * MIB, transcendentals=pairs
        ),
    )(*args)


def projections(embed_weight, embed_bias, norm_gain, w_query, w_key, w_value, w_velocity):
    width = w_query.shape[1]
    heads = width // HEAD_DIM
    latent, features = embed_weight.shape
    embed = jnp.concatenate(
        [
            embed_weight.astype(F32),
            embed_bias[None],
            jnp.zeros((DEPTH - latent - 1, features), F32),
        ],
        axis=0,
    )
    embed = embed - embed.mean(1, keepdims=True)
    gram = lax.dot_general(embed, embed, (((1,), (1,)), ((), ())), precision=HI) / features
    gained = embed * norm_gain
    high = gained.astype(BF)
    low = (gained - high.astype(F32)).astype(BF)
    joined = jnp.dot(
        jnp.concatenate([high, low], axis=0),
        jnp.concatenate([w_query, w_key, w_value], axis=1),
        preferred_element_type=F32,
    )
    joined = (joined[:DEPTH] + joined[DEPTH:]).reshape(DEPTH, 3, heads, HEAD_DIM)
    scale = HEAD_DIM ** (-0.5) * math.log2(math.e)
    forms = jnp.einsum("ehf,dhf->hed", joined[:, 1], joined[:, 0] * scale, precision=HI)
    outs = jnp.einsum(
        "ehf,hfc->hec",
        joined[:, 2],
        w_velocity.astype(F32).reshape(heads, HEAD_DIM, -1),
        precision=HI,
    )
    return gram, jnp.concatenate([outs, forms], axis=-1).astype(BF)


def copy_for_each(x, axis):
    copies = jnp.broadcast_to(x, (lax.axis_size(axis), *x.shape))
    return lax.all_to_all(copies, axis, split_axis=0, concat_axis=0, tiled=True)


def on_device(
    feats,
    conv_one,
    bias_one,
    conv_two,
    bias_two,
    patch_weight,
    patch_bias,
    embed_weight,
    embed_bias,
    norm_gain,
    w_query,
    w_key,
    w_value,
    w_velocity,
):
    rows, width, chans = feats.shape[1:]
    gram, maps = projections(
        embed_weight, embed_bias, norm_gain, w_query, w_key, w_value, w_velocity
    )
    maps = lax.all_gather(maps, "ba", axis=0, tiled=True)
    n_heads = maps.shape[0]

    halo = neighbours(feats[0], 0)
    first = conv_call(first_kernel, halo, conv_one, [bias_one[None]], (rows, width, chans))
    halo = neighbours(first, 0)
    tokens = rows * width // 4
    latents = conv_call(
        second_kernel,
        halo,
        conv_two,
        [bias_two[None], patch_weight, patch_bias[None]],
        (tokens, patch_bias.shape[0]),
    )

    ones = jnp.ones((1, tokens), F32)
    spare = jnp.zeros((DEPTH - TILE - 2, tokens), F32)
    columns = jnp.concatenate([latents.astype(F32).T, ones, 0 * ones, spare], axis=0)
    spread = (columns * jnp.dot(gram, columns, precision=HI)).sum(0, keepdims=True)
    rstd = lax.rsqrt(jnp.maximum(spread, 0.0) + 1e-05)
    own = jnp.concatenate([(columns * rstd)[: TILE + 1], ones, spare], axis=0).astype(BF)

    block = copy_for_each(own, "ba")
    count = lax.axis_size("aa")
    inner = count // 2
    blocks = [block]
    for dx, dz in ((0, 1), (0, 3), (1, 0), (0, 2), (1, 1), (1, 3), (1, 2)):
        pairs = [
            (x * inner + z, (x + dx) % 2 * inner + (z + dz) % inner)
            for x in range(2)
            for z in range(inner)
        ]
        blocks.append(lax.ppermute(block, "aa", pairs))

    forms = maps[:, :, TILE:].reshape(n_heads * DEPTH, DEPTH)
    queries = jnp.dot(forms, columns.astype(BF), preferred_element_type=F32) * rstd
    queries = queries.astype(BF).reshape(n_heads, DEPTH, tokens)

    state = attend_call(queries, blocks[:1], None, None, 8)
    state = attend_call(queries, blocks[1:2], state, None, 8)
    state = attend_call(queries, blocks[2:4], state, None, 8)
    attended = attend_call(queries, blocks[4:], state, blocks, 8)
    outs = maps[:, :, :TILE].reshape(n_heads * DEPTH, TILE)
    return lax.dot_general(
        attended.reshape(n_heads * DEPTH, tokens), outs, TN, preferred_element_type=F32
    )


def solution(mesh):
    return jax.shard_map(
        on_device,
        mesh=mesh,
        in_specs=(
            P("aa", "ba", None, None),
            P(),
            P(),
            P(),
            P(),
            P(),
            P(),
            P(),
            P(),
            P(),
            P(None, "ba"),
            P(None, "ba"),
            P(None, "ba"),
            P("ba", None),
        ),
        out_specs=P(("aa", "ba"), None),
        check_vma=False,
    )
```

```python
import functools
import math

import jax
import jax.numpy as jnp
from jax import lax
from jax.experimental import pallas as pl
from jax.experimental.pallas import tpu as pltpu
from jax.sharding import PartitionSpec as P

HEAD_DIM = 64
BF = jnp.bfloat16
F32 = jnp.float32
DEPTH = 144
TILE = 128
SAMPLE = 2
MIB = 2**20
TN = (((0,), (0,)), ((), ()))
HI = lax.Precision.HIGHEST


def gelu(x):
    return 0.5 * x * (1.0 + lax.erf(x * (1.0 / math.sqrt(2.0))))


def neighbours(block):
    na, nb = lax.axis_size("aa"), lax.axis_size("ba")

    def shift(x, axis, count, by):
        pairs = [(i, i + by) for i in range(count) if 0 <= i + by < count]
        return lax.ppermute(x, axis, pairs)

    before = shift(block, "aa", na, 1)
    after = shift(block, "aa", na, -1)
    up = shift(jnp.stack([before[-1], block[-1], after[-1]]), "ba", nb, 1)
    down = shift(jnp.stack([before[0], block[0], after[0]]), "ba", nb, -1)
    return (before, block, after, up, down)


def conv_taps(refs, w_ref, pad_ref, acc_ref):
    step = pl.program_id(0)
    rows, width, chans = refs[1].shape

    @pl.when(step == 0)
    def _():
        for t in range(3):
            pad_ref[t, 0:width] = refs[3][t]
            for r in range(rows):
                pad_ref[t, (r + 1) * width : (r + 2) * width] = refs[t][r]
            pad_ref[t, (rows + 1) * width : (rows + 2) * width] = refs[4][t]

    for w in range(3):
        total = jnp.dot(pad_ref[step, 0 : rows * width], w_ref[0, 0, w], preferred_element_type=F32)
        for r in (1, 2):
            total += jnp.dot(
                pad_ref[step, r * width : (r + rows) * width],
                w_ref[0, r, w],
                preferred_element_type=F32,
            )

        @pl.when(step == 0)
        def _():
            acc_ref[w] = total

        @pl.when(step > 0)
        def _():
            acc_ref[w] += total


def conv_sum(acc_ref, bias_ref, width):
    count = acc_ref.shape[1]
    at = lax.broadcasted_iota(jnp.int32, (count, 1), 0) % width
    left = jnp.where(at == 0, 0.0, pltpu.roll(acc_ref[0], 1, 0))
    right = jnp.where(at == width - 1, 0.0, pltpu.roll(acc_ref[2], count - 1, 0))
    return left + acc_ref[1] + right + bias_ref[...]


def first_kernel(*refs):
    halo, (w_ref, bias_ref, out_ref, pad_ref, acc_ref) = refs[:5], refs[5:]
    conv_taps(halo, w_ref, pad_ref, acc_ref)

    @pl.when(pl.program_id(0) == 2)
    def _():
        rows, width, chans = out_ref.shape
        out_ref[...] = gelu(conv_sum(acc_ref, bias_ref, width)).astype(BF).reshape(rows, width, chans)


def second_kernel(*refs):
    halo, (w_ref, bias_ref, pw_ref, pb_ref, out_ref, pad_ref, acc_ref) = refs[:5], refs[5:]
    conv_taps(halo, w_ref, pad_ref, acc_ref)

    @pl.when(pl.program_id(0) == 2)
    def _():
        rows, width, chans = halo[1].shape
        half = width // 2
        first = halo[1][...].reshape(rows * width, chans).astype(F32)
        second = (first + gelu(conv_sum(acc_ref, bias_ref, width))).astype(BF)
        r = lax.broadcasted_iota(jnp.int32, (width, width), 0)
        c = lax.broadcasted_iota(jnp.int32, (width, width), 1)
        picks = (c == jnp.where(r < half, 2 * r, 2 * r - (width - 1))).astype(BF)
        for e in range(rows // 2):
            total = pb_ref[...] + jnp.zeros((half, pb_ref.shape[1]), F32)
            for a in range(2):
                at = (2 * e + a) * width
                sorted_row = jnp.dot(
                    picks, second[at : at + width], preferred_element_type=F32
                ).astype(BF)
                for k in range(2):
                    total += jnp.dot(
                        sorted_row[k * half : (k + 1) * half],
                        pw_ref[a, k],
                        preferred_element_type=F32,
                    )
            out_ref[e * half : (e + 1) * half] = total.astype(BF)


def conv_call(kernel, halo, weight, extras, out_shape):
    rows, width, chans = halo[1].shape
    whole = [pl.BlockSpec(memory_space=pltpu.VMEM)]
    return pl.pallas_call(
        kernel,
        grid=(3,),
        in_specs=whole * 5
        + [pl.BlockSpec((1, 3, 3, chans, chans), lambda i: (i, 0, 0, 0, 0))]
        + whole * len(extras),
        out_specs=pl.BlockSpec(memory_space=pltpu.VMEM),
        out_shape=jax.ShapeDtypeStruct(out_shape, BF),
        scratch_shapes=[
            pltpu.VMEM((3, (rows + 2) * width, chans), BF),
            pltpu.VMEM((3, rows * width, chans), F32),
        ],
        compiler_params=pltpu.CompilerParams(vmem_limit_bytes=32 * MIB),
        cost_estimate=pl.CostEstimate(
            flops=2 * 27 * rows * width * chans * chans,
            bytes_accessed=2 * 27 * chans * chans,
            transcendentals=0,
        ),
    )(*halo, weight, *extras)


def side(tiles):
    return jnp.concatenate(tiles, axis=1)


def attend_kernel(n_blocks, start, finish, heads, *refs):
    q_ref, *rest = refs
    blocks, rest = rest[:n_blocks], rest[n_blocks:]
    if not start:
        (m_in, o_in, *rest) = rest
    if finish:
        n_all = len(rest) - 3
        everything, (out_ref, held, sem) = rest[:n_all], rest[n_all:]
    else:
        m_out, out_ref = rest
    query = side([q_ref[h] for h in range(heads)])

    def scores(tiles):
        return lax.dot_general(tiles, query, TN, preferred_element_type=F32)

    if start:
        sample = side([blocks[0][i] for i in range(SAMPLE)])
        shift = scores(sample).max(0, keepdims=True)
        total = jnp.zeros((DEPTH, heads * TILE), F32)
    else:
        shift = m_in[...]
        total = side([o_in[h] for h in range(heads)])
    for block in blocks:
        keys = side([block[i] for i in range(block.shape[0])])
        probs = jnp.exp2(scores(keys) - shift).astype(BF)
        total = total + jnp.dot(keys, probs, preferred_element_type=F32)
    if not finish:
        m_out[...] = shift
        for h in range(heads):
            out_ref[h] = total[:, h * TILE : (h + 1) * TILE]
        return

    def store(sums):
        scaled = (sums / sums[TILE + 1 : TILE + 2]).astype(BF)
        for h in range(heads):
            out_ref[h] = scaled[:, h * TILE : (h + 1) * TILE]

    store(total)
    largest = jnp.where(total[TILE + 1 : TILE + 2] < 2.0**100, 0.0, 1.0).max()

    @pl.when(largest > 0.5)
    def _():
        state = (
            jnp.full((1, heads * TILE), -1e38, F32),
            jnp.zeros((DEPTH, heads * TILE), F32),
        )
        for source in everything:
            copy = pltpu.make_async_copy(source, held, sem)
            copy.start()
            copy.wait()

            def one_tile(i, state):
                best, sums = state
                keys = held[i]
                s = scores(keys)
                peak = jnp.maximum(best, s.max(0, keepdims=True))
                probs = jnp.exp2(s - peak).astype(BF)
                sums = sums * jnp.exp2(best - peak) + jnp.dot(
                    keys, probs, preferred_element_type=F32
                )
                return peak, sums

            state = lax.fori_loop(0, held.shape[0], one_tile, state)
        store(state[1])


def attend_call(queries, blocks, state, everything, heads):
    n_heads = queries.shape[0]
    start, finish = state is None, everything is not None
    per_q = pl.BlockSpec((heads, DEPTH, TILE), lambda i: (i, 0, 0))
    per_m = pl.BlockSpec((1, heads * TILE), lambda i: (0, i))
    whole = pl.BlockSpec(memory_space=pltpu.VMEM)
    args, specs = [queries, *blocks], [per_q] + [whole] * len(blocks)
    if not start:
        args += list(state)
        specs += [per_m, per_q]
    scratch = []
    if finish:
        args += everything
        specs += [pl.BlockSpec(memory_space=pl.ANY)] * len(everything)
        out_specs = per_q
        out_shape = jax.ShapeDtypeStruct(queries.shape, BF)
        scratch = [pltpu.VMEM(blocks[0].shape, BF), pltpu.SemaphoreType.DMA(())]
    else:
        out_specs = [per_m, per_q]
        out_shape = [
            jax.ShapeDtypeStruct((1, n_heads * TILE), F32),
            jax.ShapeDtypeStruct(queries.shape, F32),
        ]
    pairs = n_heads * TILE * sum(b.shape[0] for b in blocks) * TILE
    return pl.pallas_call(
        functools.partial(attend_kernel, len(blocks), start, finish, heads),
        grid=(n_heads // heads,),
        in_specs=specs,
        out_specs=out_specs,
        out_shape=out_shape,
        scratch_shapes=scratch,
        compiler_params=pltpu.CompilerParams(vmem_limit_bytes=58 * MIB),
        cost_estimate=pl.CostEstimate(
            flops=pairs * 1024, bytes_accessed=4 * MIB, transcendentals=pairs
        ),
    )(*args)


def projections(embed_weight, embed_bias, norm_gain, w_query, w_key, w_value, w_velocity):
    width = w_query.shape[1]
    heads = width // HEAD_DIM
    latent, features = embed_weight.shape
    embed = jnp.concatenate(
        [
            embed_weight.astype(F32),
            embed_bias[None],
            jnp.zeros((DEPTH - latent - 1, features), F32),
        ],
        axis=0,
    )
    embed = embed - embed.mean(1, keepdims=True)
    gram = lax.dot_general(embed, embed, (((1,), (1,)), ((), ())), precision=HI) / features
    gained = embed * norm_gain
    high = gained.astype(BF)
    low = (gained - high.astype(F32)).astype(BF)
    joined = jnp.dot(
        jnp.concatenate([high, low], axis=0),
        jnp.concatenate([w_query, w_key, w_value], axis=1),
        preferred_element_type=F32,
    )
    joined = (joined[:DEPTH] + joined[DEPTH:]).reshape(DEPTH, 3, heads, HEAD_DIM)
    scale = HEAD_DIM ** (-0.5) * math.log2(math.e)
    forms = jnp.einsum("ehf,dhf->hed", joined[:, 1], joined[:, 0] * scale, precision=HI)
    outs = jnp.einsum(
        "ehf,hfc->hec",
        joined[:, 2],
        w_velocity.astype(F32).reshape(heads, HEAD_DIM, -1),
        precision=HI,
    )
    return gram, jnp.concatenate([outs, forms], axis=-1).astype(BF)


def copy_for_each(x, axis):
    copies = jnp.broadcast_to(x, (lax.axis_size(axis), *x.shape))
    return lax.all_to_all(copies, axis, split_axis=0, concat_axis=0, tiled=True)


def on_device(
    feats,
    conv_one,
    bias_one,
    conv_two,
    bias_two,
    patch_weight,
    patch_bias,
    embed_weight,
    embed_bias,
    norm_gain,
    w_query,
    w_key,
    w_value,
    w_velocity,
):
    rows, width, chans = feats.shape[1:]
    gram, maps = projections(
        embed_weight, embed_bias, norm_gain, w_query, w_key, w_value, w_velocity
    )
    peers = lax.axis_size("ba")
    far_bit = peers // 2
    while far_bit:
        pairs = [(i, i ^ far_bit) for i in range(peers)]
        maps = jnp.concatenate([maps, lax.ppermute(maps, "ba", pairs)], axis=0)
        far_bit //= 2
    n_heads = maps.shape[0]

    halo = neighbours(feats[0])
    first = conv_call(first_kernel, halo, conv_one, [bias_one[None]], (rows, width, chans))
    halo = neighbours(first)
    tokens = rows * width // 4
    latents = conv_call(
        second_kernel,
        halo,
        conv_two,
        [bias_two[None], patch_weight, patch_bias[None]],
        (tokens, patch_bias.shape[0]),
    )

    ones = jnp.ones((1, tokens), F32)
    spare = jnp.zeros((DEPTH - TILE - 2, tokens), F32)
    columns = jnp.concatenate([latents.astype(F32).T, ones, 0 * ones, spare], axis=0)
    spread = (columns * jnp.dot(gram, columns, precision=HI)).sum(0, keepdims=True)
    rstd = lax.rsqrt(jnp.maximum(spread, 0.0) + 1e-05)
    own = jnp.concatenate([(columns * rstd)[: TILE + 1], ones, spare], axis=0).astype(BF)

    block = copy_for_each(own, "ba")
    count = lax.axis_size("aa")
    inner = count // 2
    def send(source, dx, dz):
        pairs = [
            (x * inner + z, (x + dx) % 2 * inner + (z + dz) % inner)
            for x in range(2)
            for z in range(inner)
        ]
        return lax.ppermute(source, "aa", pairs)

    near = [send(block, 0, 1), send(block, 0, 3), send(block, 1, 0)]

    forms = maps[:, :, TILE:].reshape(n_heads * DEPTH, DEPTH)
    queries = jnp.dot(forms, columns.astype(BF), preferred_element_type=F32) * rstd
    queries = queries.astype(BF).reshape(n_heads, DEPTH, tokens)

    state = attend_call(queries, [block], None, None, 8)
    block, near, state = lax.optimization_barrier((block, near, state))
    far = [
        send(block, 1, 2),
        send(near[0], 0, 1),
        send(near[0], 1, 0),
        send(near[2], 0, 3),
    ]
    state = attend_call(queries, near, state, None, 8)
    attended = attend_call(queries, far, state, [block, *near, *far], 8)
    outs = maps[:, :, :TILE].reshape(n_heads * DEPTH, TILE)
    return lax.dot_general(
        attended.reshape(n_heads * DEPTH, tokens), outs, TN, preferred_element_type=F32
    )


def solution(mesh):
    return jax.shard_map(
        on_device,
        mesh=mesh,
        in_specs=(
            P("aa", "ba", None, None),
            P(),
            P(),
            P(),
            P(),
            P(),
            P(),
            P(),
            P(),
            P(),
            P(None, "ba"),
            P(None, "ba"),
            P(None, "ba"),
            P("ba", None),
        ),
        out_specs=P(("aa", "ba"), None),
        check_vma=False,
    )
```

```python
import functools
import math

import jax
import jax.numpy as jnp
from jax import lax
from jax.experimental import pallas as pl
from jax.experimental.pallas import tpu as pltpu
from jax.sharding import PartitionSpec as P

HEAD_DIM = 64
BF = jnp.bfloat16
F32 = jnp.float32
DEPTH = 144
TILE = 128
SAMPLE = 2
MIB = 2**20
TN = (((0,), (0,)), ((), ()))
HI = lax.Precision.HIGHEST


def gelu(x):
    return 0.5 * x * (1.0 + lax.erf(x * (1.0 / math.sqrt(2.0))))


def shifted(x, axis, by):
    count = lax.axis_size(axis)
    return lax.ppermute(x, axis, [(i, i + by) for i in range(count) if 0 <= i + by < count])


def frames_around(block):
    return shifted(block, "aa", 1), shifted(block, "aa", -1)


def rows_around(before, block, after):
    up = shifted(jnp.stack([before[-1], block[-1], after[-1]]), "ba", 1)
    down = shifted(jnp.stack([before[0], block[0], after[0]]), "ba", -1)
    return (before, block, after, up, down)


def from_peer(x, axis, bit):
    return lax.ppermute(x, axis, [(i, i ^ bit) for i in range(lax.axis_size(axis))])


def conv_taps(refs, w_ref, pad_ref, acc_ref):
    rows, width, chans = refs[1].shape
    for t in range(3):
        pad_ref[t, 0:width] = refs[3][t]
        for r in range(rows):
            pad_ref[t, (r + 1) * width : (r + 2) * width] = refs[t][r]
        pad_ref[t, (rows + 1) * width : (rows + 2) * width] = refs[4][t]
    for w in range(3):
        total = None
        for t in range(3):
            for r in range(3):
                part = jnp.dot(
                    pad_ref[t, r * width : (r + rows) * width],
                    w_ref[t, r, w],
                    preferred_element_type=F32,
                )
                total = part if total is None else total + part
        acc_ref[w] = total


def conv_sum(acc_ref, bias_ref, width):
    count = acc_ref.shape[1]
    at = lax.broadcasted_iota(jnp.int32, (count, 1), 0) % width
    left = jnp.where(at == 0, 0.0, pltpu.roll(acc_ref[0], 1, 0))
    right = jnp.where(at == width - 1, 0.0, pltpu.roll(acc_ref[2], count - 1, 0))
    return left + acc_ref[1] + right + bias_ref[...]


def first_kernel(*refs):
    halo, (w_ref, bias_ref, out_ref, pad_ref, acc_ref) = refs[:5], refs[5:]
    conv_taps(halo, w_ref, pad_ref, acc_ref)

    rows, width, chans = out_ref.shape
    out_ref[...] = gelu(conv_sum(acc_ref, bias_ref, width)).astype(BF).reshape(rows, width, chans)


def second_kernel(*refs):
    halo, rest = refs[:5], refs[5:]
    w_ref, bias_ref, pw_ref, pb_ref, gram_ref, keys_ref, pad_ref, acc_ref = rest
    conv_taps(halo, w_ref, pad_ref, acc_ref)

    rows, width, chans = halo[1].shape
    half = width // 2
    first = halo[1][...].reshape(rows * width, chans).astype(F32)
    second = (first + gelu(conv_sum(acc_ref, bias_ref, width))).astype(BF)
    r = lax.broadcasted_iota(jnp.int32, (width, width), 0)
    c = lax.broadcasted_iota(jnp.int32, (width, width), 1)
    picks = (c == jnp.where(r < half, 2 * r, 2 * r - (width - 1))).astype(BF)
    latents = []
    for e in range(rows // 2):
        total = pb_ref[...] + jnp.zeros((half, pb_ref.shape[1]), F32)
        for a in range(2):
            at = (2 * e + a) * width
            sorted_row = jnp.dot(
                picks, second[at : at + width], preferred_element_type=F32
            ).astype(BF)
            for k in range(2):
                total += jnp.dot(
                    sorted_row[k * half : (k + 1) * half],
                    pw_ref[a, k],
                    preferred_element_type=F32,
                )
        latents.append(total.astype(BF).astype(F32))
    latents = jnp.concatenate(latents, axis=0).T
    at = lax.broadcasted_iota(jnp.int32, (DEPTH - TILE, TILE), 0)
    columns = jnp.concatenate([latents, jnp.where(at == 0, 1.0, 0.0)], axis=0)
    spread = jnp.dot(gram_ref[...], columns, precision=HI, preferred_element_type=F32)
    spread = (spread * columns).sum(0, keepdims=True)
    rstd = lax.rsqrt(jnp.maximum(spread, 0.0) + 1e-05)
    keys = (columns * rstd).astype(BF)
    tail = jnp.where(at == 0, rstd, jnp.where(at == 1, 1.0, 0.0)).astype(BF)
    for i in range(keys_ref.shape[0]):
        keys_ref[i, 0:TILE] = keys[0:TILE]
        keys_ref[i, TILE:DEPTH] = tail


def conv_call(kernel, halo, weight, extras, out_shapes):
    rows, width, chans = halo[1].shape
    whole = [pl.BlockSpec(memory_space=pltpu.VMEM)]
    return pl.pallas_call(
        kernel,
        in_specs=whole * (len(halo) + 1 + len(extras)),
        out_specs=whole * len(out_shapes),
        out_shape=[jax.ShapeDtypeStruct(*shape) for shape in out_shapes],
        scratch_shapes=[
            pltpu.VMEM((3, (rows + 2) * width, chans), BF),
            pltpu.VMEM((3, rows * width, chans), F32),
        ],
        compiler_params=pltpu.CompilerParams(vmem_limit_bytes=32 * MIB),
        cost_estimate=pl.CostEstimate(
            flops=2 * 27 * rows * width * chans * chans,
            bytes_accessed=2 * 27 * chans * chans,
            transcendentals=0,
        ),
    )(*halo, weight, *extras)


def side(tiles):
    return jnp.concatenate(tiles, axis=1)


def chosen(even, even_ref, odd_ref, h):
    return jnp.where(even, even_ref[h].astype(F32), odd_ref[h].astype(F32)).astype(BF)


def attend_kernel(n_blocks, start, finish, heads, *refs):
    even = pl.program_id(0) % 2 == 0
    if start:
        even_ref, odd_ref, place_ref, *rest = refs
    elif finish:
        q_ref, even_ref, odd_ref, *rest = refs
    else:
        q_ref, *rest = refs
    blocks, rest = rest[:n_blocks], rest[n_blocks:]
    if not start:
        (m_in, o_in, *rest) = rest
    if finish:
        n_all = len(rest) - 3
        earlier, (out_ref, held, sem) = rest[:n_all], rest[n_all:]
    elif start:
        q_out, m_out, out_ref = rest
    else:
        m_out, out_ref = rest

    if start:
        tile = blocks[0][place_ref[pl.program_id(0) // 2]]
        query = []
        for h in range(heads):
            form = chosen(even, even_ref.at[:, :, TILE:], odd_ref.at[:, :, TILE:], h)
            query.append(jnp.dot(form, tile, preferred_element_type=F32).astype(BF))
            q_out[h] = query[h]
        query = side(query)
    else:
        query = side([q_ref[h] for h in range(heads)])

    def scores(tiles):
        return lax.dot_general(tiles, query, TN, preferred_element_type=F32)

    if start:
        sample = side([blocks[0][i] for i in range(SAMPLE)])
        shift = scores(sample).max(0, keepdims=True)
        total = jnp.zeros((DEPTH, heads * TILE), F32)
    else:
        shift = m_in[...]
        total = side([o_in[h] for h in range(heads)])
    for block in blocks:
        keys = side([block[i] for i in range(block.shape[0])])
        probs = jnp.exp2(scores(keys) - shift).astype(BF)
        total = total + jnp.dot(keys, probs, preferred_element_type=F32)
    if not finish:
        m_out[...] = shift
        for h in range(heads):
            out_ref[h] = total[:, h * TILE : (h + 1) * TILE]
        return

    @pl.when(pl.program_id(0) == 0)
    def _():
        out_ref[...] = jnp.zeros_like(out_ref)

    def deliver(sums):
        scaled = (sums / sums[TILE + 1 : TILE + 2]).astype(BF)
        moved = jnp.zeros((TILE, TILE), F32)
        for h in range(heads):
            moved += lax.dot_general(
                scaled[:, h * TILE : (h + 1) * TILE],
                chosen(even, even_ref, odd_ref, h),
                TN,
                preferred_element_type=F32,
            )
        out_ref[...] += moved

    largest = jnp.where(total[TILE + 1 : TILE + 2] < 2.0**100, 0.0, 1.0).max()

    @pl.when(largest < 0.5)
    def _():
        deliver(total)

    @pl.when(largest > 0.5)
    def _():
        state = (
            jnp.full((1, heads * TILE), -1e38, F32),
            jnp.zeros((DEPTH, heads * TILE), F32),
        )

        def over(ref, state):
            def one_tile(i, state):
                best, sums = state
                keys = ref[i]
                s = scores(keys)
                peak = jnp.maximum(best, s.max(0, keepdims=True))
                probs = jnp.exp2(s - peak).astype(BF)
                sums = sums * jnp.exp2(best - peak) + jnp.dot(
                    keys, probs, preferred_element_type=F32
                )
                return peak, sums

            return lax.fori_loop(0, ref.shape[0], one_tile, state)

        for source in earlier:
            copy = pltpu.make_async_copy(source, held, sem)
            copy.start()
            copy.wait()
            state = over(held, state)
        for block in blocks:
            state = over(block, state)
        deliver(state[1])


def attend_call(sources, blocks, state, earlier=None, tokens=None):
    start, finish = state is None, earlier is not None
    heads = sources[0].shape[0] if start else sources[1].shape[0] if finish else 8
    n_heads = 4 * heads
    steps, offset = (2, 2 * tokens) if finish else (4, 0)
    per_q = pl.BlockSpec((heads, DEPTH, TILE), lambda i: (i + offset, 0, 0))
    per_m = pl.BlockSpec((1, heads * TILE), lambda i: (0, i + offset))
    whole = pl.BlockSpec(memory_space=pltpu.VMEM)
    args = [*sources, *blocks]
    if start:
        specs = [whole] * 2 + [pl.BlockSpec(memory_space=pltpu.SMEM)]
    elif finish:
        specs = [per_q] + [pl.BlockSpec((heads, DEPTH, TILE), lambda i: (0, 0, 0))] * 2
    else:
        specs = [per_q]
    specs = specs + [whole] * len(blocks)
    if not start:
        args += list(state)
        specs += [per_m, per_q]
    shape = (n_heads, DEPTH, TILE)
    scratch = []
    if finish:
        args += earlier
        specs += [pl.BlockSpec(memory_space=pl.ANY)] * len(earlier)
        out_specs = whole
        out_shape = jax.ShapeDtypeStruct((TILE, TILE), F32)
        scratch = [pltpu.VMEM(blocks[0].shape, BF), pltpu.SemaphoreType.DMA(())]
    else:
        out_specs = [per_m, per_q]
        out_shape = [
            jax.ShapeDtypeStruct((1, n_heads * TILE), F32),
            jax.ShapeDtypeStruct(shape, F32),
        ]
        if start:
            out_specs = [per_q] + out_specs
            out_shape = [jax.ShapeDtypeStruct(shape, BF)] + out_shape
    pairs = steps * heads * TILE * sum(b.shape[0] for b in blocks) * TILE
    return pl.pallas_call(
        functools.partial(attend_kernel, len(blocks), start, finish, heads),
        grid=(steps,),
        in_specs=specs,
        out_specs=out_specs,
        out_shape=out_shape,
        scratch_shapes=scratch,
        compiler_params=pltpu.CompilerParams(vmem_limit_bytes=44 * MIB),
        cost_estimate=pl.CostEstimate(
            flops=pairs * 1024, bytes_accessed=4 * MIB, transcendentals=pairs
        ),
    )(*args)


def projections(embed_weight, embed_bias, norm_gain, w_query, w_key, w_value, w_velocity):
    width = w_query.shape[1]
    heads = width // HEAD_DIM
    latent, features = embed_weight.shape
    embed = jnp.concatenate(
        [
            embed_weight.astype(F32),
            embed_bias[None],
            jnp.zeros((DEPTH - latent - 1, features), F32),
        ],
        axis=0,
    )
    embed = embed - embed.mean(1, keepdims=True)
    gram = lax.dot_general(embed, embed, (((1,), (1,)), ((), ())), precision=HI) / features
    gained = embed * norm_gain
    high = gained.astype(BF)
    low = (gained - high.astype(F32)).astype(BF)
    joined = jnp.dot(
        jnp.concatenate([high, low], axis=0),
        jnp.concatenate([w_query, w_key, w_value], axis=1),
        preferred_element_type=F32,
    )
    joined = (joined[:DEPTH] + joined[DEPTH:]).reshape(DEPTH, 3, heads, HEAD_DIM)
    scale = HEAD_DIM ** (-0.5) * math.log2(math.e)
    forms = jnp.einsum("ehf,dhf->hed", joined[:, 1], joined[:, 0] * scale, precision=HI)
    outs = jnp.einsum(
        "ehf,hfc->hec",
        joined[:, 2],
        w_velocity.astype(F32).reshape(heads, HEAD_DIM, -1),
        precision=HI,
    )
    return gram, jnp.concatenate([outs, forms], axis=-1).astype(BF)


def on_device(
    feats,
    conv_one,
    bias_one,
    conv_two,
    bias_two,
    patch_weight,
    patch_bias,
    embed_weight,
    embed_bias,
    norm_gain,
    w_query,
    w_key,
    w_value,
    w_velocity,
):
    rows, width, chans = feats.shape[1:]
    gram, maps = projections(
        embed_weight, embed_bias, norm_gain, w_query, w_key, w_value, w_velocity
    )
    peers = lax.axis_size("ba")
    bits = [peers >> k for k in range(1, peers.bit_length())]

    block = feats[0]
    before, after, maps = lax.optimization_barrier((*frames_around(block), maps))
    halo = rows_around(before, block, after)
    others = from_peer(maps, "ba", bits[0])
    for bit in bits[1:-1]:
        maps = jnp.concatenate([maps, others], axis=0)
        others = from_peer(maps, "ba", bit)
    maps = [maps, others]
    (first,) = conv_call(
        first_kernel, halo, conv_one, [bias_one[None]], [((rows, width, chans), BF)]
    )
    before, after = frames_around(first)
    halo = rows_around(before, first, after)
    tokens = rows * width // 4
    (keys,) = conv_call(
        second_kernel,
        halo,
        conv_two,
        [bias_two[None], patch_weight, patch_bias[None], gram],
        [((peers, DEPTH, tokens), BF)],
    )
    block = lax.all_to_all(keys, "ba", 0, 0, tiled=True)
    count = lax.axis_size("aa")
    inner = count // 2
    def send(source, dx, dz):
        pairs = [
            (x * inner + z, (x + dx) % 2 * inner + (z + dz) % inner)
            for x in range(2)
            for z in range(inner)
        ]
        return lax.ppermute(source, "aa", pairs)

    near = [send(block, 0, 1), send(block, 0, 3), send(block, 1, 0)]

    me = lax.axis_index("ba")
    places = jnp.stack([me, me ^ 1]).astype(jnp.int32)
    queries, *state = attend_call([*maps, places], [block], None)
    block, near, state = lax.optimization_barrier((block, near, state))
    far = [
        send(block, 1, 2),
        send(near[0], 0, 1),
        send(near[0], 1, 0),
        send(near[2], 0, 3),
    ]
    state = attend_call([queries], near, state)
    earlier = [block, *near]
    theirs = attend_call([queries, *maps], far, state, earlier, 1)
    theirs, state = lax.optimization_barrier((theirs, state))
    theirs = from_peer(theirs, "ba", bits[-1])
    return attend_call([queries, *maps], far, state, earlier, 0) + theirs


def solution(mesh):
    return jax.shard_map(
        on_device,
        mesh=mesh,
        in_specs=(
            P("aa", "ba", None, None),
            P(),
            P(),
            P(),
            P(),
            P(),
            P(),
            P(),
            P(),
            P(),
            P(None, "ba"),
            P(None, "ba"),
            P(None, "ba"),
            P("ba", None),
        ),
        out_specs=P(("aa", "ba"), None),
        check_vma=False,
    )
```

```python
import functools
import math

import jax
import jax.numpy as jnp
from jax import lax
from jax.experimental import pallas as pl
from jax.experimental.pallas import tpu as pltpu
from jax.sharding import PartitionSpec as P

HEAD_DIM = 64
BF = jnp.bfloat16
F32 = jnp.float32
DEPTH = 144
TILE = 128
SAMPLE = 2
MIB = 2**20
TN = (((0,), (0,)), ((), ()))
HI = lax.Precision.HIGHEST


def gelu(x):
    return 0.5 * x * (1.0 + lax.erf(x * (1.0 / math.sqrt(2.0))))


def shifted(x, axis, by):
    count = lax.axis_size(axis)
    return lax.ppermute(x, axis, [(i, i + by) for i in range(count) if 0 <= i + by < count])


def frames_around(block):
    return shifted(block, "aa", 1), shifted(block, "aa", -1)


def rows_around(before, block, after):
    up = shifted(jnp.stack([before[-1], block[-1], after[-1]]), "ba", 1)
    down = shifted(jnp.stack([before[0], block[0], after[0]]), "ba", -1)
    return (before, block, after, up, down)


def from_peer(x, axis, bit):
    return lax.ppermute(x, axis, [(i, i ^ bit) for i in range(lax.axis_size(axis))])


def conv_taps(refs, w_ref, pad_ref, acc_ref):
    rows, width, chans = refs[1].shape
    for t in range(3):
        pad_ref[t, 0:width] = refs[3][t]
        for r in range(rows):
            pad_ref[t, (r + 1) * width : (r + 2) * width] = refs[t][r]
        pad_ref[t, (rows + 1) * width : (rows + 2) * width] = refs[4][t]
    for w in range(3):
        total = None
        for t in range(3):
            for r in range(3):
                part = jnp.dot(
                    pad_ref[t, r * width : (r + rows) * width],
                    w_ref[t, r, w],
                    preferred_element_type=F32,
                )
                total = part if total is None else total + part
        acc_ref[w] = total


def conv_sum(acc_ref, bias_ref, width):
    count = acc_ref.shape[1]
    at = lax.broadcasted_iota(jnp.int32, (count, 1), 0) % width
    left = jnp.where(at == 0, 0.0, pltpu.roll(acc_ref[0], 1, 0))
    right = jnp.where(at == width - 1, 0.0, pltpu.roll(acc_ref[2], count - 1, 0))
    return left + acc_ref[1] + right + bias_ref[...]


def first_kernel(*refs):
    halo, (w_ref, bias_ref, out_ref, pad_ref, acc_ref) = refs[:5], refs[5:]
    conv_taps(halo, w_ref, pad_ref, acc_ref)

    rows, width, chans = out_ref.shape
    out_ref[...] = gelu(conv_sum(acc_ref, bias_ref, width)).astype(BF).reshape(rows, width, chans)


def second_kernel(*refs):
    halo, rest = refs[:5], refs[5:]
    w_ref, bias_ref, pw_ref, pb_ref, gram_ref, keys_ref, pad_ref, acc_ref = rest
    conv_taps(halo, w_ref, pad_ref, acc_ref)

    rows, width, chans = halo[1].shape
    half = width // 2
    first = halo[1][...].reshape(rows * width, chans).astype(F32)
    second = (first + gelu(conv_sum(acc_ref, bias_ref, width))).astype(BF)
    r = lax.broadcasted_iota(jnp.int32, (width, width), 0)
    c = lax.broadcasted_iota(jnp.int32, (width, width), 1)
    picks = (c == jnp.where(r < half, 2 * r, 2 * r - (width - 1))).astype(BF)
    latents = []
    for e in range(rows // 2):
        total = pb_ref[...] + jnp.zeros((half, pb_ref.shape[1]), F32)
        for a in range(2):
            at = (2 * e + a) * width
            sorted_row = jnp.dot(
                picks, second[at : at + width], preferred_element_type=F32
            ).astype(BF)
            for k in range(2):
                total += jnp.dot(
                    sorted_row[k * half : (k + 1) * half],
                    pw_ref[a, k],
                    preferred_element_type=F32,
                )
        latents.append(total.astype(BF).astype(F32))
    latents = jnp.concatenate(latents, axis=0).T
    at = lax.broadcasted_iota(jnp.int32, (DEPTH - TILE, TILE), 0)
    columns = jnp.concatenate([latents, jnp.where(at == 0, 1.0, 0.0)], axis=0)
    spread = jnp.dot(gram_ref[...], columns, precision=HI, preferred_element_type=F32)
    spread = (spread * columns).sum(0, keepdims=True)
    rstd = lax.rsqrt(jnp.maximum(spread, 0.0) + 1e-05)
    keys = (columns * rstd).astype(BF)
    tail = jnp.where(at == 0, rstd, jnp.where(at == 1, 1.0, 0.0)).astype(BF)
    for i in range(keys_ref.shape[0]):
        keys_ref[i, 0:TILE] = keys[0:TILE]
        keys_ref[i, TILE:DEPTH] = tail


def conv_call(kernel, halo, weight, extras, out_shapes):
    rows, width, chans = halo[1].shape
    whole = [pl.BlockSpec(memory_space=pltpu.VMEM)]
    return pl.pallas_call(
        kernel,
        in_specs=whole * (len(halo) + 1 + len(extras)),
        out_specs=whole * len(out_shapes),
        out_shape=[jax.ShapeDtypeStruct(*shape) for shape in out_shapes],
        scratch_shapes=[
            pltpu.VMEM((3, (rows + 2) * width, chans), BF),
            pltpu.VMEM((3, rows * width, chans), F32),
        ],
        compiler_params=pltpu.CompilerParams(vmem_limit_bytes=32 * MIB),
        cost_estimate=pl.CostEstimate(
            flops=2 * 27 * rows * width * chans * chans,
            bytes_accessed=2 * 27 * chans * chans,
            transcendentals=0,
        ),
    )(*halo, weight, *extras)


def side(tiles):
    return jnp.concatenate(tiles, axis=1)


def chosen(even, even_ref, odd_ref, h):
    return jnp.where(even, even_ref[h].astype(F32), odd_ref[h].astype(F32)).astype(BF)


def attend_kernel(n_blocks, start, finish, heads, *refs):
    even = pl.program_id(0) % 2 == 0
    if start:
        even_ref, odd_ref, place_ref, *rest = refs
    elif finish:
        q_ref, even_ref, odd_ref, *rest = refs
    else:
        q_ref, *rest = refs
    blocks, rest = rest[:n_blocks], rest[n_blocks:]
    if not start:
        (m_in, o_in, *rest) = rest
    if finish:
        n_all = len(rest) - 4
        earlier, (own_ref, other_ref, held, sem) = rest[:n_all], rest[n_all:]
    elif start:
        q_out, m_out, out_ref = rest
    else:
        m_out, out_ref = rest

    if start:
        tile = blocks[0][place_ref[pl.program_id(0) // 2]]
        query = []
        for h in range(heads):
            form = chosen(even, even_ref.at[:, :, TILE:], odd_ref.at[:, :, TILE:], h)
            query.append(jnp.dot(form, tile, preferred_element_type=F32).astype(BF))
            q_out[h] = query[h]
        query = side(query)
    else:
        query = side([q_ref[h] for h in range(heads)])

    def scores(tiles):
        return lax.dot_general(tiles, query, TN, preferred_element_type=F32)

    if start:
        sample = side([blocks[0][i] for i in range(SAMPLE)])
        shift = scores(sample).max(0, keepdims=True)
        total = jnp.zeros((DEPTH, heads * TILE), F32)
    else:
        shift = m_in[...]
        total = side([o_in[h] for h in range(heads)])
    for block in blocks:
        keys = side([block[i] for i in range(block.shape[0])])
        probs = jnp.exp2(scores(keys) - shift).astype(BF)
        total = total + jnp.dot(keys, probs, preferred_element_type=F32)
    if not finish:
        m_out[...] = shift
        for h in range(heads):
            out_ref[h] = total[:, h * TILE : (h + 1) * TILE]
        return

    @pl.when(pl.program_id(0) == 0)
    def _():
        own_ref[...] = jnp.zeros_like(own_ref)
        other_ref[...] = jnp.zeros_like(other_ref)

    def deliver(sums):
        scaled = (sums / sums[TILE + 1 : TILE + 2]).astype(BF)
        moved = jnp.zeros((TILE, TILE), F32)
        for h in range(heads):
            moved += lax.dot_general(
                scaled[:, h * TILE : (h + 1) * TILE],
                chosen(even, even_ref, odd_ref, h),
                TN,
                preferred_element_type=F32,
            )

        @pl.when(pl.program_id(0) < 2)
        def _():
            own_ref[...] += moved

        @pl.when(pl.program_id(0) >= 2)
        def _():
            other_ref[...] += moved

    largest = jnp.where(total[TILE + 1 : TILE + 2] < 2.0**100, 0.0, 1.0).max()

    @pl.when(largest < 0.5)
    def _():
        deliver(total)

    @pl.when(largest > 0.5)
    def _():
        state = (
            jnp.full((1, heads * TILE), -1e38, F32),
            jnp.zeros((DEPTH, heads * TILE), F32),
        )

        def over(ref, state):
            def one_tile(i, state):
                best, sums = state
                keys = ref[i]
                s = scores(keys)
                peak = jnp.maximum(best, s.max(0, keepdims=True))
                probs = jnp.exp2(s - peak).astype(BF)
                sums = sums * jnp.exp2(best - peak) + jnp.dot(
                    keys, probs, preferred_element_type=F32
                )
                return peak, sums

            return lax.fori_loop(0, ref.shape[0], one_tile, state)

        for source in earlier:
            copy = pltpu.make_async_copy(source, held, sem)
            copy.start()
            copy.wait()
            state = over(held, state)
        for block in blocks:
            state = over(block, state)
        deliver(state[1])


def attend_call(sources, blocks, state, earlier=None):
    start, finish = state is None, earlier is not None
    heads = sources[0].shape[0] if start else sources[1].shape[0] if finish else 8
    n_heads = 4 * heads
    steps = 4
    per_q = pl.BlockSpec((heads, DEPTH, TILE), lambda i: (i, 0, 0))
    per_m = pl.BlockSpec((1, heads * TILE), lambda i: (0, i))
    whole = pl.BlockSpec(memory_space=pltpu.VMEM)
    args = [*sources, *blocks]
    if start:
        specs = [whole] * 2 + [pl.BlockSpec(memory_space=pltpu.SMEM)]
    elif finish:
        specs = [per_q] + [pl.BlockSpec((heads, DEPTH, TILE), lambda i: (0, 0, 0))] * 2
    else:
        specs = [per_q]
    specs = specs + [whole] * len(blocks)
    if not start:
        args += list(state)
        specs += [per_m, per_q]
    shape = (n_heads, DEPTH, TILE)
    scratch = []
    if finish:
        args += earlier
        specs += [pl.BlockSpec(memory_space=pl.ANY)] * len(earlier)
        out_specs = [whole] * 2
        out_shape = [jax.ShapeDtypeStruct((TILE, TILE), F32)] * 2
        scratch = [pltpu.VMEM(blocks[0].shape, BF), pltpu.SemaphoreType.DMA(())]
    else:
        out_specs = [per_m, per_q]
        out_shape = [
            jax.ShapeDtypeStruct((1, n_heads * TILE), F32),
            jax.ShapeDtypeStruct(shape, F32),
        ]
        if start:
            out_specs = [per_q] + out_specs
            out_shape = [jax.ShapeDtypeStruct(shape, BF)] + out_shape
    pairs = steps * heads * TILE * sum(b.shape[0] for b in blocks) * TILE
    return pl.pallas_call(
        functools.partial(attend_kernel, len(blocks), start, finish, heads),
        grid=(steps,),
        in_specs=specs,
        out_specs=out_specs,
        out_shape=out_shape,
        scratch_shapes=scratch,
        compiler_params=pltpu.CompilerParams(vmem_limit_bytes=44 * MIB),
        cost_estimate=pl.CostEstimate(
            flops=pairs * 1024, bytes_accessed=4 * MIB, transcendentals=pairs
        ),
    )(*args)


def projections(embed_weight, embed_bias, norm_gain, w_query, w_key, w_value, w_velocity):
    width = w_query.shape[1]
    heads = width // HEAD_DIM
    latent, features = embed_weight.shape
    embed = jnp.concatenate(
        [
            embed_weight.astype(F32),
            embed_bias[None],
            jnp.zeros((DEPTH - latent - 1, features), F32),
        ],
        axis=0,
    )
    embed = embed - embed.mean(1, keepdims=True)
    gram = lax.dot_general(embed, embed, (((1,), (1,)), ((), ())), precision=HI) / features
    gained = embed * norm_gain
    high = gained.astype(BF)
    low = (gained - high.astype(F32)).astype(BF)
    joined = jnp.dot(
        jnp.concatenate([high, low], axis=0),
        jnp.concatenate([w_query, w_key, w_value], axis=1),
        preferred_element_type=F32,
    )
    joined = (joined[:DEPTH] + joined[DEPTH:]).reshape(DEPTH, 3, heads, HEAD_DIM)
    scale = HEAD_DIM ** (-0.5) * math.log2(math.e)
    forms = jnp.einsum("ehf,dhf->hed", joined[:, 1], joined[:, 0] * scale, precision=HI)
    outs = jnp.einsum(
        "ehf,hfc->hec",
        joined[:, 2],
        w_velocity.astype(F32).reshape(heads, HEAD_DIM, -1),
        precision=HI,
    )
    return gram, jnp.concatenate([outs, forms], axis=-1).astype(BF)


def on_device(
    feats,
    conv_one,
    bias_one,
    conv_two,
    bias_two,
    patch_weight,
    patch_bias,
    embed_weight,
    embed_bias,
    norm_gain,
    w_query,
    w_key,
    w_value,
    w_velocity,
):
    rows, width, chans = feats.shape[1:]
    gram, maps = projections(
        embed_weight, embed_bias, norm_gain, w_query, w_key, w_value, w_velocity
    )
    peers = lax.axis_size("ba")
    bits = [peers >> k for k in range(1, peers.bit_length())]

    block = feats[0]
    before, after, maps = lax.optimization_barrier((*frames_around(block), maps))
    halo = rows_around(before, block, after)
    others = from_peer(maps, "ba", bits[0])
    for bit in bits[1:-1]:
        maps = jnp.concatenate([maps, others], axis=0)
        others = from_peer(maps, "ba", bit)
    maps = [maps, others]
    (first,) = conv_call(
        first_kernel, halo, conv_one, [bias_one[None]], [((rows, width, chans), BF)]
    )
    before, after = frames_around(first)
    halo = rows_around(before, first, after)
    tokens = rows * width // 4
    (keys,) = conv_call(
        second_kernel,
        halo,
        conv_two,
        [bias_two[None], patch_weight, patch_bias[None], gram],
        [((peers, DEPTH, tokens), BF)],
    )
    block = lax.all_to_all(keys, "ba", 0, 0, tiled=True)
    count = lax.axis_size("aa")
    inner = count // 2
    def send(source, dx, dz):
        pairs = [
            (x * inner + z, (x + dx) % 2 * inner + (z + dz) % inner)
            for x in range(2)
            for z in range(inner)
        ]
        return lax.ppermute(source, "aa", pairs)

    near = [send(block, 0, 1), send(block, 0, 3), send(block, 1, 0)]

    me = lax.axis_index("ba")
    places = jnp.stack([me, me ^ 1]).astype(jnp.int32)
    queries, *state = attend_call([*maps, places], [block], None)
    block, near, state = lax.optimization_barrier((block, near, state))
    far = [
        send(block, 1, 2),
        send(near[0], 0, 1),
        send(near[0], 1, 0),
        send(near[2], 0, 3),
    ]
    state = attend_call([queries], near, state)
    earlier = [block, *near]
    own, theirs = attend_call([queries, *maps], far, state, earlier)
    return own + from_peer(theirs, "ba", bits[-1])


def solution(mesh):
    return jax.shard_map(
        on_device,
        mesh=mesh,
        in_specs=(
            P("aa", "ba", None, None),
            P(),
            P(),
            P(),
            P(),
            P(),
            P(),
            P(),
            P(),
            P(),
            P(None, "ba"),
            P(None, "ba"),
            P(None, "ba"),
            P("ba", None),
        ),
        out_specs=P(("aa", "ba"), None),
        check_vma=False,
    )
```

```python
import functools
import math

import jax
import jax.numpy as jnp
from jax import lax
from jax.experimental import pallas as pl
from jax.experimental.pallas import tpu as pltpu
from jax.sharding import PartitionSpec as P

HEAD_DIM = 64
BF = jnp.bfloat16
F32 = jnp.float32
DEPTH = 144
TILE = 128
SAMPLE = 2
MIB = 2**20
TN = (((0,), (0,)), ((), ()))
HI = lax.Precision.HIGHEST


def gelu(x):
    return 0.5 * x * (1.0 + lax.erf(x * (1.0 / math.sqrt(2.0))))


def shifted(x, axis, by):
    count = lax.axis_size(axis)
    return lax.ppermute(x, axis, [(i, i + by) for i in range(count) if 0 <= i + by < count])


def frames_around(block):
    return shifted(block, "aa", 1), shifted(block, "aa", -1)


def rows_around(before, block, after):
    up = shifted(jnp.stack([before[-1], block[-1], after[-1]]), "ba", 1)
    down = shifted(jnp.stack([before[0], block[0], after[0]]), "ba", -1)
    return (before, block, after, up, down)


def from_peer(x, axis, bit):
    return lax.ppermute(x, axis, [(i, i ^ bit) for i in range(lax.axis_size(axis))])


def conv_taps(refs, w_ref, pad_ref, acc_ref):
    rows, width, chans = refs[1].shape
    for t in range(3):
        pad_ref[t, 0:width] = refs[3][t]
        for r in range(rows):
            pad_ref[t, (r + 1) * width : (r + 2) * width] = refs[t][r]
        pad_ref[t, (rows + 1) * width : (rows + 2) * width] = refs[4][t]
    for w in range(3):
        total = None
        for t in range(3):
            for r in range(3):
                part = jnp.dot(
                    pad_ref[t, r * width : (r + rows) * width],
                    w_ref[t, r, w],
                    preferred_element_type=F32,
                )
                total = part if total is None else total + part
        acc_ref[w] = total


def conv_sum(acc_ref, bias_ref, width):
    count = acc_ref.shape[1]
    at = lax.broadcasted_iota(jnp.int32, (count, 1), 0) % width
    left = jnp.where(at == 0, 0.0, pltpu.roll(acc_ref[0], 1, 0))
    right = jnp.where(at == width - 1, 0.0, pltpu.roll(acc_ref[2], count - 1, 0))
    return left + acc_ref[1] + right + bias_ref[...]


def first_kernel(*refs):
    halo, (w_ref, bias_ref, out_ref, pad_ref, acc_ref) = refs[:5], refs[5:]
    conv_taps(halo, w_ref, pad_ref, acc_ref)

    rows, width, chans = out_ref.shape
    out_ref[...] = gelu(conv_sum(acc_ref, bias_ref, width)).astype(BF).reshape(rows, width, chans)


def second_kernel(*refs):
    halo, rest = refs[:5], refs[5:]
    w_ref, bias_ref, pw_ref, pb_ref, gram_ref, keys_ref, pad_ref, acc_ref = rest
    conv_taps(halo, w_ref, pad_ref, acc_ref)

    rows, width, chans = halo[1].shape
    half = width // 2
    first = halo[1][...].reshape(rows * width, chans).astype(F32)
    second = (first + gelu(conv_sum(acc_ref, bias_ref, width))).astype(BF)
    r = lax.broadcasted_iota(jnp.int32, (width, width), 0)
    c = lax.broadcasted_iota(jnp.int32, (width, width), 1)
    picks = (c == jnp.where(r < half, 2 * r, 2 * r - (width - 1))).astype(BF)
    latents = []
    for e in range(rows // 2):
        total = pb_ref[...] + jnp.zeros((half, pb_ref.shape[1]), F32)
        for a in range(2):
            at = (2 * e + a) * width
            sorted_row = jnp.dot(
                picks, second[at : at + width], preferred_element_type=F32
            ).astype(BF)
            for k in range(2):
                total += jnp.dot(
                    sorted_row[k * half : (k + 1) * half],
                    pw_ref[a, k],
                    preferred_element_type=F32,
                )
        latents.append(total.astype(BF).astype(F32))
    latents = jnp.concatenate(latents, axis=0).T
    at = lax.broadcasted_iota(jnp.int32, (DEPTH - TILE, TILE), 0)
    columns = jnp.concatenate([latents, jnp.where(at == 0, 1.0, 0.0)], axis=0)
    spread = jnp.dot(gram_ref[...], columns, precision=HI, preferred_element_type=F32)
    spread = (spread * columns).sum(0, keepdims=True)
    rstd = lax.rsqrt(jnp.maximum(spread, 0.0) + 1e-05)
    keys = (columns * rstd).astype(BF)
    tail = jnp.where(at == 0, rstd, jnp.where(at == 1, 1.0, 0.0)).astype(BF)
    for i in range(keys_ref.shape[0]):
        keys_ref[i, 0:TILE] = keys[0:TILE]
        keys_ref[i, TILE:DEPTH] = tail


def conv_call(kernel, halo, weight, extras, out_shapes):
    rows, width, chans = halo[1].shape
    whole = [pl.BlockSpec(memory_space=pltpu.VMEM)]
    return pl.pallas_call(
        kernel,
        in_specs=whole * (len(halo) + 1 + len(extras)),
        out_specs=whole * len(out_shapes),
        out_shape=[jax.ShapeDtypeStruct(*shape) for shape in out_shapes],
        scratch_shapes=[
            pltpu.VMEM((3, (rows + 2) * width, chans), BF),
            pltpu.VMEM((3, rows * width, chans), F32),
        ],
        compiler_params=pltpu.CompilerParams(vmem_limit_bytes=32 * MIB),
        cost_estimate=pl.CostEstimate(
            flops=2 * 27 * rows * width * chans * chans,
            bytes_accessed=2 * 27 * chans * chans,
            transcendentals=0,
        ),
    )(*halo, weight, *extras)


def side(tiles):
    return jnp.concatenate(tiles, axis=1)


def chosen(even, even_ref, odd_ref, h):
    return jnp.where(even, even_ref[h].astype(F32), odd_ref[h].astype(F32)).astype(BF)


def attend_kernel(n_blocks, start, finish, heads, *refs):
    even = pl.program_id(0) % 2 == 0
    if start:
        even_ref, odd_ref, place_ref, *rest = refs
    elif finish:
        q_ref, even_ref, odd_ref, *rest = refs
    else:
        q_ref, *rest = refs
    blocks, rest = rest[:n_blocks], rest[n_blocks:]
    if not start:
        (m_in, o_in, *rest) = rest
    if finish:
        n_all = len(rest) - 4
        earlier, (own_ref, other_ref, held, sem) = rest[:n_all], rest[n_all:]
    elif start:
        q_out, m_out, out_ref = rest
    else:
        m_out, out_ref = rest

    if start:
        tile = blocks[0][place_ref[pl.program_id(0) // 2]]
        query = []
        for h in range(heads):
            form = chosen(even, even_ref.at[:, :, TILE:], odd_ref.at[:, :, TILE:], h)
            query.append(jnp.dot(form, tile, preferred_element_type=F32).astype(BF))
            q_out[h] = query[h]
        query = side(query)
    else:
        query = side([q_ref[h] for h in range(heads)])

    def scores(tiles):
        return lax.dot_general(tiles, query, TN, preferred_element_type=F32)

    if start:
        sample = side([blocks[0][i] for i in range(SAMPLE)])
        shift = scores(sample).max(0, keepdims=True)
        total = jnp.zeros((DEPTH, heads * TILE), F32)
    else:
        shift = m_in[...]
        total = side([o_in[h] for h in range(heads)])
    for block in blocks:
        keys = side([block[i] for i in range(block.shape[0])])
        probs = jnp.exp2(scores(keys) - shift).astype(BF)
        total = total + jnp.dot(keys, probs, preferred_element_type=F32)
    if not finish:
        m_out[...] = shift
        for h in range(heads):
            out_ref[h] = total[:, h * TILE : (h + 1) * TILE]
        return

    @pl.when(pl.program_id(0) == 0)
    def _():
        own_ref[...] = jnp.zeros_like(own_ref)
        other_ref[...] = jnp.zeros_like(other_ref)

    def deliver(sums):
        scaled = (sums / sums[TILE + 1 : TILE + 2]).astype(BF)
        moved = jnp.zeros((TILE, TILE), F32)
        for h in range(heads):
            moved += lax.dot_general(
                scaled[:, h * TILE : (h + 1) * TILE],
                chosen(even, even_ref, odd_ref, h),
                TN,
                preferred_element_type=F32,
            )

        @pl.when(pl.program_id(0) < 2)
        def _():
            own_ref[...] += moved

        @pl.when(pl.program_id(0) >= 2)
        def _():
            other_ref[...] += moved

    largest = jnp.where(total[TILE + 1 : TILE + 2] < 2.0**100, 0.0, 1.0).max()

    @pl.when(largest < 0.5)
    def _():
        deliver(total)

    @pl.when(largest > 0.5)
    def _():
        state = (
            jnp.full((1, heads * TILE), -1e38, F32),
            jnp.zeros((DEPTH, heads * TILE), F32),
        )

        def over(ref, state):
            def one_tile(i, state):
                best, sums = state
                keys = ref[i]
                s = scores(keys)
                peak = jnp.maximum(best, s.max(0, keepdims=True))
                probs = jnp.exp2(s - peak).astype(BF)
                sums = sums * jnp.exp2(best - peak) + jnp.dot(
                    keys, probs, preferred_element_type=F32
                )
                return peak, sums

            return lax.fori_loop(0, ref.shape[0], one_tile, state)

        for source in earlier:
            copy = pltpu.make_async_copy(source, held, sem)
            copy.start()
            copy.wait()
            state = over(held, state)
        for block in blocks:
            state = over(block, state)
        deliver(state[1])


def attend_call(sources, blocks, state, earlier=None):
    start, finish = state is None, earlier is not None
    heads = sources[0].shape[0] if start else sources[1].shape[0] if finish else 8
    n_heads = 4 * heads
    steps = 4
    per_q = pl.BlockSpec((heads, DEPTH, TILE), lambda i: (i, 0, 0))
    per_m = pl.BlockSpec((1, heads * TILE), lambda i: (0, i))
    whole = pl.BlockSpec(memory_space=pltpu.VMEM)
    args = [*sources, *blocks]
    if start:
        specs = [whole] * 2 + [pl.BlockSpec(memory_space=pltpu.SMEM)]
    elif finish:
        specs = [per_q] + [pl.BlockSpec((heads, DEPTH, TILE), lambda i: (0, 0, 0))] * 2
    else:
        specs = [per_q]
    specs = specs + [whole] * len(blocks)
    if not start:
        args += list(state)
        specs += [per_m, per_q]
    shape = (n_heads, DEPTH, TILE)
    scratch = []
    if finish:
        args += earlier
        specs += [pl.BlockSpec(memory_space=pl.ANY)] * len(earlier)
        out_specs = [whole] * 2
        out_shape = [jax.ShapeDtypeStruct((TILE, TILE), F32)] * 2
        scratch = [pltpu.VMEM(blocks[0].shape, BF), pltpu.SemaphoreType.DMA(())]
    else:
        out_specs = [per_m, per_q]
        out_shape = [
            jax.ShapeDtypeStruct((1, n_heads * TILE), F32),
            jax.ShapeDtypeStruct(shape, F32),
        ]
        if start:
            out_specs = [per_q] + out_specs
            out_shape = [jax.ShapeDtypeStruct(shape, BF)] + out_shape
    pairs = steps * heads * TILE * sum(b.shape[0] for b in blocks) * TILE
    return pl.pallas_call(
        functools.partial(attend_kernel, len(blocks), start, finish, heads),
        grid=(steps,),
        in_specs=specs,
        out_specs=out_specs,
        out_shape=out_shape,
        scratch_shapes=scratch,
        compiler_params=pltpu.CompilerParams(vmem_limit_bytes=32 * MIB),
        cost_estimate=pl.CostEstimate(
            flops=pairs * 1024, bytes_accessed=4 * MIB, transcendentals=pairs
        ),
    )(*args)


def projections(embed_weight, embed_bias, norm_gain, w_query, w_key, w_value, w_velocity):
    width = w_query.shape[1]
    heads = width // HEAD_DIM
    latent, features = embed_weight.shape
    embed = jnp.concatenate(
        [
            embed_weight.astype(F32),
            embed_bias[None],
            jnp.zeros((DEPTH - latent - 1, features), F32),
        ],
        axis=0,
    )
    embed = embed - embed.mean(1, keepdims=True)
    gram = lax.dot_general(embed, embed, (((1,), (1,)), ((), ())), precision=HI) / features
    gained = embed * norm_gain
    high = gained.astype(BF)
    low = (gained - high.astype(F32)).astype(BF)
    joined = jnp.dot(
        jnp.concatenate([high, low], axis=0),
        jnp.concatenate([w_query, w_key, w_value], axis=1),
        preferred_element_type=F32,
    )
    joined = (joined[:DEPTH] + joined[DEPTH:]).reshape(DEPTH, 3, heads, HEAD_DIM)
    scale = HEAD_DIM ** (-0.5) * math.log2(math.e)
    forms = jnp.einsum("ehf,dhf->hed", joined[:, 1], joined[:, 0] * scale, precision=HI)
    outs = jnp.einsum(
        "ehf,hfc->hec",
        joined[:, 2],
        w_velocity.astype(F32).reshape(heads, HEAD_DIM, -1),
        precision=HI,
    )
    return gram, jnp.concatenate([outs, forms], axis=-1).astype(BF)


def on_device(
    feats,
    conv_one,
    bias_one,
    conv_two,
    bias_two,
    patch_weight,
    patch_bias,
    embed_weight,
    embed_bias,
    norm_gain,
    w_query,
    w_key,
    w_value,
    w_velocity,
):
    rows, width, chans = feats.shape[1:]
    gram, maps = projections(
        embed_weight, embed_bias, norm_gain, w_query, w_key, w_value, w_velocity
    )
    peers = lax.axis_size("ba")
    bits = [peers >> k for k in range(1, peers.bit_length())]

    block = feats[0]
    before, after, maps = lax.optimization_barrier((*frames_around(block), maps))
    halo = rows_around(before, block, after)
    others = from_peer(maps, "ba", bits[0])
    for bit in bits[1:-1]:
        maps = jnp.concatenate([maps, others], axis=0)
        others = from_peer(maps, "ba", bit)
    maps = [maps, others]
    (first,) = conv_call(
        first_kernel, halo, conv_one, [bias_one[None]], [((rows, width, chans), BF)]
    )
    before, after = frames_around(first)
    halo = rows_around(before, first, after)
    tokens = rows * width // 4
    (keys,) = conv_call(
        second_kernel,
        halo,
        conv_two,
        [bias_two[None], patch_weight, patch_bias[None], gram],
        [((peers, DEPTH, tokens), BF)],
    )
    block = lax.all_to_all(keys, "ba", 0, 0, tiled=True)
    count = lax.axis_size("aa")
    inner = count // 2
    def send(source, dx, dz):
        pairs = [
            (x * inner + z, (x + dx) % 2 * inner + (z + dz) % inner)
            for x in range(2)
            for z in range(inner)
        ]
        return lax.ppermute(source, "aa", pairs)

    near = [send(block, 0, 1), send(block, 0, 3), send(block, 1, 0)]

    me = lax.axis_index("ba")
    places = jnp.stack([me, me ^ 1]).astype(jnp.int32)
    queries, *state = attend_call([*maps, places], [block], None)
    block, near, state = lax.optimization_barrier((block, near, state))
    far = [
        send(block, 1, 2),
        send(near[0], 0, 1),
        send(near[0], 1, 0),
        send(near[2], 0, 3),
    ]
    state = attend_call([queries], near, state)
    earlier = [block, *near]
    own, theirs = attend_call([queries, *maps], far, state, earlier)
    return own + from_peer(theirs, "ba", bits[-1])


def solution(mesh):
    return jax.shard_map(
        on_device,
        mesh=mesh,
        in_specs=(
            P("aa", "ba", None, None),
            P(),
            P(),
            P(),
            P(),
            P(),
            P(),
            P(),
            P(),
            P(),
            P(None, "ba"),
            P(None, "ba"),
            P(None, "ba"),
            P("ba", None),
        ),
        out_specs=P(("aa", "ba"), None),
        check_vma=False,
    )
```
